256 devices in a mesh: spin: 2 (over core), band: 128 (over y, z, x).
Axes of the slice: x: 4, y: 4, z: 8, core: 2. Of those that a mesh axis runs over, the one named last changes fastest.
Arguments:
- orbitals: float32 [2, 128, 32768], P('spin', 'band'), may hold values from -15 to 15
- potential: float32 [32768], replicated, may hold values from -6 to 6
Outputs:
- updated: float32 [2, 128, 32768], P('spin', 'band')
- residual: float32 [2, 128, 32768], P('spin', 'band')
The draws below stay inside these ranges and needn't reach their ends.
All inputs are finite; a program needn't handle non-finite values.
Results may differ from the reference program's by a relative error of at most 0.0003.
Values sent between devices are 32-bit elements; how exact they have to be, the bound alone decides.
No kernel may reach another device: no remote copies, remote signals or barrier semaphores. Data moves between devices by JAX's collectives and lax.ppermute only.
A program may use at most 128 MiB of HBM per device.

```python
import math
import jax
import jax.numpy as jnp
from jax import lax

SPINS = 2
GRID = 32
G = 32768
BAND_DEV = 1
NB = 128


def draw_orbitals(key, part):
    sample_key, band_key, cell_key = jax.random.split(key, 3)
    band_scale = jnp.exp(jax.random.uniform(band_key, (SPINS, NB, 1), jnp.float32, math.log(0.7), math.log(1.4)))
    planes = (jnp.arange(G, dtype=jnp.int32) // (GRID * GRID)).astype(jnp.float32)
    cell_scale = 0.6 * jnp.exp(planes * (math.log(3.0) / GRID) + jax.random.uniform(cell_key, (G,), jnp.float32, -0.15, 0.15))
    samples = jnp.clip(jax.random.normal(sample_key, (SPINS, NB, G), jnp.float32), -5.0, 5.0)
    return samples * band_scale * cell_scale


def scatter_about(own_key, dims, spread, reach, kind=jnp.bfloat16):
    return jnp.clip(spread * jax.random.normal(own_key, dims, jnp.float32), -reach, reach).astype(kind)


def setup_inputs(seed: int = 0) -> dict:
    keys = jax.random.split(jax.random.key(seed), 3)
    return {
        "orbitals": draw_orbitals(jax.random.fold_in(keys[2], 71), 0),
        "potential": scatter_about(keys[1], (G,), 1.0, 6.0, jnp.float32),
    }


screen_square = 0.04
hartree_weight = 0.03125
mixing = 0.25
step_length = 0.1


def cas_table(points):
    indices = jnp.arange(points, dtype=jnp.int32)
    phase_index = (indices[:, None] * indices[None, :]) % points
    angles = phase_index.astype(jnp.float32) * (2.0 * math.pi / points)
    return jnp.cos(angles) + jnp.sin(angles)


def wave_squares(points):
    indices = jnp.arange(points, dtype=jnp.int32)
    folded = jnp.where(indices < points // 2, indices, indices - points).astype(jnp.float32)
    wavenumber = folded * (math.pi / points)
    squares = wavenumber * wavenumber
    summed = squares[:, None, None] + squares[None, :, None] + squares[None, None, :]
    return summed.reshape(-1)


def hartley(signal, table):
    points = table.shape[0]
    leading = signal.shape[:-1]
    cube_field = signal.reshape((-1, points, points, points))
    for axis_turn in range(3):
        cube_field = jnp.einsum("ka,sabc->sbck", table, cube_field, precision=lax.Precision.HIGHEST)
    return cube_field.reshape(leading + (points ** 3,))


def screened(signal, table, kernel):
    return hartley(kernel * hartley(signal, table), table) / kernel.shape[0]


def reference(orbitals, potential):
    table = cas_table(GRID)
    wave_square = wave_squares(GRID)
    kernel = jnp.where(wave_square > 0, 1.0 / (wave_square + screen_square), 0.0)
    volume = orbitals.shape[2]
    density = jnp.sum(orbitals * orbitals, axis=(0, 1))
    local_field = potential + hartree_weight * screened(density, table, kernel)
    blocks = NB // BAND_DEV
    grouped = orbitals.reshape(SPINS, blocks, BAND_DEV, volume)

    def exchange_block(flat_index):
        spin_index = flat_index // blocks
        block_index = flat_index % blocks
        resident = grouped[spin_index, block_index]
        accumulated = jnp.zeros((BAND_DEV, volume), jnp.float32)
        for offset in (-2, -1, 0, 1, 2):
            partner = grouped[spin_index, (block_index + offset) % blocks]
            pair_field = (resident[:, None, :] * partner[None, :, :]).reshape(-1, volume)
            fields = screened(pair_field, table, kernel).reshape(BAND_DEV, BAND_DEV, volume)
            accumulated = accumulated - jnp.sum(fields * partner[None, :, :], axis=1)
        return accumulated

    exchange_term = lax.map(exchange_block, jnp.arange(SPINS * blocks, dtype=jnp.int32))
    exchange_term = exchange_term.reshape(SPINS, NB, volume)
    kinetic = hartley(0.5 * wave_square * hartley(orbitals, table), table) / volume
    gradient = kinetic + local_field * orbitals + mixing * exchange_term
    first_correlation = jnp.einsum("sjr,sir->sji", orbitals, gradient, precision=lax.Precision.HIGHEST) / volume
    projected = gradient - jnp.einsum("sji,sjr->sir", first_correlation, orbitals, precision=lax.Precision.HIGHEST)
    second_correlation = jnp.einsum("sjr,sir->sji", orbitals, projected, precision=lax.Precision.HIGHEST) / volume
    residual = projected - jnp.einsum("sji,sjr->sir", second_correlation, orbitals, precision=lax.Precision.HIGHEST)
    return orbitals - step_length * residual, residual
```

```python
import math

import jax
import jax.numpy as jnp
import ml_dtypes
import numpy as np
from jax import lax
from jax.experimental import pallas as pl
from jax.experimental.pallas import tpu as pltpu
from jax.sharding import Mesh
from jax.sharding import PartitionSpec as P

GRID = 32
PLANE = GRID * GRID
CELLS = GRID**3
LANES = 128
ROWS = CELLS // LANES
SPLIT = PLANE // LANES

SCREEN_SQUARE = 0.04
HARTREE_WEIGHT = 0.03125
MIXING = 0.25
STEP_LENGTH = 0.1

BANDS = ("y", "z", "x")
GRID_X = 4
SLAB = ("y", "x")
GATHER = ("z",)

f32 = jnp.float32
bf16 = jnp.bfloat16


def halves(value):
    high = value.astype(ml_dtypes.bfloat16)
    low = (value - high.astype(np.float64)).astype(ml_dtypes.bfloat16)
    return high, low


def constants():
    indices = np.arange(GRID)
    angles = (indices[:, None] * indices[None, :] % GRID) * (2.0 * math.pi / GRID)
    table = np.cos(angles) + np.sin(angles)
    joined = np.stack(halves(np.kron(table, table)))
    lines = np.stack(halves(np.kron(np.eye(4), table)))
    return jnp.asarray(joined), jnp.asarray(lines)


def wave_square():
    planes = lax.broadcasted_iota(jnp.int32, (GRID, PLANE), 0)
    cells = lax.broadcasted_iota(jnp.int32, (GRID, PLANE), 1)

    def square(index):
        wave = jnp.where(index < GRID // 2, index, index - GRID).astype(f32) * (math.pi / GRID)
        return wave * wave

    return square(planes) + square(cells // GRID) + square(cells % GRID)


def screening(squares):
    kept = squares > 0
    return jnp.where(kept, 1.0 / jnp.where(kept, squares + SCREEN_SQUARE, 1.0), 0.0) * (1.0 / CELLS)


def split(value):
    high = value.astype(bf16)
    return high, (value - high.astype(f32)).astype(bf16)


def mm(left, right):
    return lax.dot_general(left, right, (((1,), (0,)), ((), ())), preferred_element_type=f32)


def mmt(left, right):
    return lax.dot_general(left, right, (((1,), (1,)), ((), ())), preferred_element_type=f32)


def product(left, right_high, right_low, multiply):
    high, low = split(left)
    rows = left.shape[0]
    both = multiply(jnp.concatenate([high, low], axis=0), right_high)
    return both[:rows] + both[rows:] + multiply(high, right_low)


def along_line(value, lines):
    rows = value.shape[0]
    line_high, line_low = lines[0, :rows, :rows], lines[1, :rows, :rows]
    high, low = split(value)
    both = mm(jnp.concatenate([line_high, line_low], axis=0), high)
    return both[:rows] + both[rows:] + mm(line_high, low)


def twice_transformed(fields, factors, joined, lines, copies):
    high, low = split(fields)
    rows = fields.shape[0]
    copies[0].wait()
    both = mm(jnp.concatenate([high, low], axis=0), joined[0])
    copies[1].wait()
    value = both[:rows] + both[rows:] + mm(high, joined[1])
    copies[2].wait()
    value = along_line(value, lines) * factors
    return along_line(product(value, joined[0], joined[1], mm), lines)


def to_planes(ref):
    return jnp.concatenate([ref[pl.ds(j, GRID, stride=SPLIT), :] for j in range(SPLIT)], axis=1)


def table_copies(joined_ref, lines_ref, joined, lines, sems):
    copies = [
        pltpu.make_async_copy(joined_ref.at[0], joined.at[0], sems.at[0]),
        pltpu.make_async_copy(joined_ref.at[1], joined.at[1], sems.at[1]),
        pltpu.make_async_copy(lines_ref, lines, sems.at[2]),
    ]
    for copy in copies:
        copy.start()
    return copies


TABLE_SCRATCH = [
    pltpu.VMEM((2, PLANE, PLANE), bf16),
    pltpu.VMEM((2, LANES, LANES), bf16),
    pltpu.SemaphoreType.DMA((3,)),
]


def own_kernel(o_ref, joined_ref, lines_ref, square_ref, start_ref, joined, lines, sems):
    copies = table_copies(joined_ref, lines_ref, joined, lines, sems)
    own = to_planes(o_ref)
    fields = jnp.concatenate([own * own, own], axis=0)
    squares = wave_square()
    factors = jnp.concatenate([screening(squares), squares * (0.5 / CELLS)], axis=0)
    fields = twice_transformed(fields, factors, joined, lines, copies)
    square, kinetic = fields[:GRID], fields[GRID:]
    start = kinetic - MIXING * square * own
    for j in range(SPLIT):
        rows = pl.ds(j, GRID, stride=SPLIT)
        start_ref[rows, :] = start[:, j * LANES : (j + 1) * LANES]
        square_ref[rows, :] = square[:, j * LANES : (j + 1) * LANES]


def pack_kernel(o_ref, square_ref, other_ref, packed_ref):
    shape = packed_ref.shape[0], packed_ref.shape[2], LANES
    packed_ref[:, 0] = o_ref[...].reshape(shape)
    packed_ref[:, 1] = (square_ref[...] + other_ref[...]).reshape(shape)


def pair_kernel(x_ref, o_ref, start_ref, below, above, second, across, corner, joined_ref, lines_ref, out_ref, joined, lines, sems):
    copies = table_copies(joined_ref, lines_ref, joined, lines, sems)
    own = to_planes(o_ref)
    below, above, second, across, corner = (to_planes(ref) for ref in (below, above, second, across, corner))
    x = x_ref[0]
    partners = [
        jnp.where(x == 0, corner, below),
        jnp.where(x == GRID_X - 1, corner, above),
        second,
        across,
    ]
    fields = jnp.concatenate([own * partner for partner in partners], axis=0)
    factors = jnp.concatenate([screening(wave_square())] * 4, axis=0)
    fields = twice_transformed(fields, factors, joined, lines, copies)
    total = sum(fields[k * GRID : (k + 1) * GRID] * partners[k] for k in range(4))
    for j in range(SPLIT):
        rows = pl.ds(j, GRID, stride=SPLIT)
        out_ref[rows, :] = start_ref[rows, :] - MIXING * total[:, j * LANES : (j + 1) * LANES]


def slab_kernel(slabs_ref, out_ref):
    bands, rows = slabs_ref.shape[0], slabs_ref.shape[2]
    out_ref[: bands * rows] = slabs_ref[:, 0].reshape(bands * rows, LANES)
    out_ref[bands * rows :] = jnp.sum(slabs_ref[:, 1], axis=0)


def correlate_kernel(g_ref, potential_ref, *refs):
    pieces, (corr_ref, g_out, oh_ref, ol_ref) = refs[:-4], refs[-4:]
    bands, rows = g_ref.shape[0], g_ref.shape[1]
    cells = bands * rows
    count = bands * len(pieces)
    squares = sum(piece[cells:, :] for piece in pieces)
    local = potential_ref[...] + HARTREE_WEIGHT * squares
    g = g_ref[...] + local[None] * pieces[0][:cells].reshape(bands, rows, LANES)
    g_out[...] = g
    for k, piece in enumerate(pieces):
        for c in range(rows):
            high, low = split(piece[pl.ds(c, bands, stride=rows), :])
            oh_ref[k * bands : (k + 1) * bands, c * LANES : (c + 1) * LANES] = high
            ol_ref[k * bands : (k + 1) * bands, c * LANES : (c + 1) * LANES] = low
    wide = jnp.concatenate([g[:, c, :] for c in range(rows)], axis=1)
    g_high, g_low = split(wide)
    high, low = oh_ref[...], ol_ref[...]
    left_high = jnp.concatenate([g_high, high], axis=0)
    left_low = jnp.concatenate([g_low, low], axis=0)
    total = mmt(left_high, high) + mmt(left_low, high) + mmt(left_high, low)
    total = total * (1.0 / CELLS)
    half = count // 2
    quarter = half // 2
    kept = bands + half
    corner = total[kept:, half:]
    corr_ref[:kept] = total[:kept]
    corr_ref[kept:] = jnp.concatenate([corner[:quarter], corner[quarter:]], axis=1)


def remove_kernel(corr_ref, g_ref, oh_ref, ol_ref, out_ref):
    bands, rows = g_ref.shape[0], g_ref.shape[1]
    corr = jnp.sum(corr_ref[...], axis=0)
    half = corr.shape[1] // 2
    kept = bands + half
    first, upper, corner = corr[:bands], corr[bands:kept], corr[kept:]
    lower = jnp.concatenate([corner[:, :half], corner[:, half:]], axis=0)
    lower = jnp.concatenate([upper[:, half:].T, lower], axis=1)
    overlap = jnp.concatenate([upper, lower], axis=0)
    s_high, s_low = split(overlap)
    weights = 2.0 * first - product(first, s_high, s_low, mm)
    taken = product(weights, oh_ref[...], ol_ref[...], mm)
    for c in range(rows):
        out_ref[:, c, :] = g_ref[:, c, :] - taken[:, c * LANES : (c + 1) * LANES]


def call(kernel, outs, args, name, tables=(), flops=1 << 30, nbytes=1 << 23):
    single = not isinstance(outs, list)
    shapes = [outs] if single else outs
    result = pl.pallas_call(
        kernel,
        out_shape=[jax.ShapeDtypeStruct(s, t) for s, t in shapes],
        in_specs=[pl.BlockSpec(memory_space=pltpu.SMEM if a.dtype == jnp.int32 else pltpu.VMEM) for a in args]
        + [pl.BlockSpec(memory_space=pltpu.HBM)] * len(tables),
        out_specs=[pl.BlockSpec(memory_space=pltpu.VMEM)] * len(shapes),
        compiler_params=pltpu.CompilerParams(vmem_limit_bytes=40 << 20),
        cost_estimate=pl.CostEstimate(flops=flops, bytes_accessed=nbytes, transcendentals=0),
        scratch_shapes=TABLE_SCRATCH if tables else [],
        name=name,
    )(*args, *tables)
    return result[0] if single else result


def exchange(x, axes):
    return lax.all_to_all(x, axes, 0, 0, tiled=True)


def gather(x, axes):
    return exchange(jnp.broadcast_to(x[None], (size(axes),) + x.shape), axes)


def size(axes):
    return math.prod(lax.axis_size(a) for a in axes)


def shifted(x, axes, by):
    peers = size(axes)
    return lax.ppermute(x, axes, [(i, (i + by) % peers) for i in range(peers)])


def per_device(orbitals, potential):
    tables = constants()
    parts = size(SLAB)
    rows = ROWS // parts
    groups = size(GATHER)

    own = orbitals.reshape(ROWS, LANES)
    below, above, second = (shifted(own, ("x",), by) for by in (1, -1, 2))
    rings = size(("y", "z"))
    toward = [-1, -1, 1, 1]
    edge = lax.ppermute(
        own,
        BANDS,
        [(g * GRID_X + x, (g + toward[x]) % rings * GRID_X + x) for g in range(rings) for x in range(GRID_X)],
    )
    square, start = call(
        own_kernel,
        [((ROWS, LANES), f32), ((ROWS, LANES), f32)],
        [own],
        "own_fields",
        tables,
    )
    other = shifted(square, ("spin",), 1)
    packed = call(pack_kernel, ((parts, 2, rows, LANES), f32), [own, square, other], "pack")
    packed, start, edge, below, above, second = lax.optimization_barrier((packed, start, edge, below, above, second))
    across = shifted(edge, ("x",), 2)
    corner = lax.ppermute(edge, "x", [(0, GRID_X - 1), (GRID_X - 1, 0)])
    slabs = exchange(packed, SLAB)
    slab = call(slab_kernel, (((parts + 1) * rows, LANES), f32), [slabs], "slab")
    pieces = [slab] + [shifted(slab, GATHER, by) for by in (1, -1, 2, -2, 3, -3, 4)]
    gradient = call(
        pair_kernel,
        ((ROWS, LANES), f32),
        [lax.axis_index("x").reshape(1), own, start, below, above, second, across, corner],
        "pair_fields",
        tables,
    )
    gradient, slab = lax.optimization_barrier((gradient, slab))
    slab_gradient = exchange(gradient.reshape(parts, rows, LANES), SLAB)
    here = lax.axis_index(SLAB)
    slab_potential = lax.dynamic_slice_in_dim(potential.reshape(ROWS, LANES), here * rows, rows, 0)
    bands = parts * groups
    corr, slab_gradient, o_high, o_low = call(
        correlate_kernel,
        [
            ((parts + 3 * bands // 4, LANES), f32),
            ((parts, rows, LANES), f32),
            ((bands, rows * LANES), bf16),
            ((bands, rows * LANES), bf16),
        ],
        [slab_gradient, slab_potential, *pieces],
        "correlations",
    )
    spread = gather(corr, SLAB)
    slab_residual = call(
        remove_kernel,
        ((parts, rows, LANES), f32),
        [spread, slab_gradient, o_high, o_low],
        "removal",
    )
    residual = exchange(slab_residual, SLAB).reshape(1, 1, CELLS)
    return orbitals - STEP_LENGTH * residual, residual


def solution(mesh):
    fine = Mesh(mesh.devices.reshape(2, 4, 8, 4), ("spin",) + BANDS)
    spec = P("spin", BANDS, None)
    return jax.shard_map(
        per_device, mesh=fine, in_specs=(spec, P()), out_specs=(spec, spec), check_vma=False
    )
```

```python
import math

import jax
import jax.numpy as jnp
import ml_dtypes
import numpy as np
from jax import lax
from jax.experimental import pallas as pl
from jax.experimental.pallas import tpu as pltpu
from jax.sharding import Mesh
from jax.sharding import PartitionSpec as P

GRID = 32
PLANE = GRID * GRID
CELLS = GRID**3
LANES = 128
ROWS = CELLS // LANES
SPLIT = PLANE // LANES

SCREEN_SQUARE = 0.04
HARTREE_WEIGHT = 0.03125
MIXING = 0.25
STEP_LENGTH = 0.1

BANDS = ("y", "zh", "zl", "x")
GRID_X = 4
SLAB = ("y", "zl", "x")
GATHER = ("zh",)

f32 = jnp.float32
bf16 = jnp.bfloat16


def halves(value):
    high = value.astype(ml_dtypes.bfloat16)
    low = (value - high.astype(np.float64)).astype(ml_dtypes.bfloat16)
    return high, low


def constants():
    indices = np.arange(GRID)
    angles = (indices[:, None] * indices[None, :] % GRID) * (2.0 * math.pi / GRID)
    table = np.cos(angles) + np.sin(angles)
    joined = np.stack(halves(np.kron(table, table)))
    lines = np.stack(halves(np.kron(np.eye(4), table)))
    return jnp.asarray(joined), jnp.asarray(lines)


def wave_square():
    planes = lax.broadcasted_iota(jnp.int32, (GRID, PLANE), 0)
    cells = lax.broadcasted_iota(jnp.int32, (GRID, PLANE), 1)

    def square(index):
        wave = jnp.where(index < GRID // 2, index, index - GRID).astype(f32) * (math.pi / GRID)
        return wave * wave

    return square(planes) + square(cells // GRID) + square(cells % GRID)


def screening(squares):
    kept = squares > 0
    return jnp.where(kept, 1.0 / jnp.where(kept, squares + SCREEN_SQUARE, 1.0), 0.0) * (1.0 / CELLS)


def split(value):
    high = value.astype(bf16)
    return high, (value - high.astype(f32)).astype(bf16)


def mm(left, right):
    return lax.dot_general(left, right, (((1,), (0,)), ((), ())), preferred_element_type=f32)


def mmt(left, right):
    return lax.dot_general(left, right, (((1,), (1,)), ((), ())), preferred_element_type=f32)


def product(left, right_high, right_low, multiply):
    high, low = split(left)
    rows = left.shape[0]
    both = multiply(jnp.concatenate([high, low], axis=0), right_high)
    return both[:rows] + both[rows:] + multiply(high, right_low)


def along_line(value, lines):
    rows = value.shape[0]
    line_high, line_low = lines[0, :rows, :rows], lines[1, :rows, :rows]
    high, low = split(value)
    both = mm(jnp.concatenate([line_high, line_low], axis=0), high)
    return both[:rows] + both[rows:] + mm(line_high, low)


def twice_transformed(fields, factors, joined, lines, copies):
    high, low = split(fields)
    rows = fields.shape[0]
    copies[0].wait()
    both = mm(jnp.concatenate([high, low], axis=0), joined[0])
    copies[1].wait()
    value = both[:rows] + both[rows:] + mm(high, joined[1])
    copies[2].wait()
    value = along_line(value, lines) * factors
    return along_line(product(value, joined[0], joined[1], mm), lines)


def to_planes(ref):
    return jnp.concatenate([ref[pl.ds(j, GRID, stride=SPLIT), :] for j in range(SPLIT)], axis=1)


def table_copies(joined_ref, lines_ref, joined, lines, sems):
    copies = [
        pltpu.make_async_copy(joined_ref.at[0], joined.at[0], sems.at[0]),
        pltpu.make_async_copy(joined_ref.at[1], joined.at[1], sems.at[1]),
        pltpu.make_async_copy(lines_ref, lines, sems.at[2]),
    ]
    for copy in copies:
        copy.start()
    return copies


TABLE_SCRATCH = [
    pltpu.VMEM((2, PLANE, PLANE), bf16),
    pltpu.VMEM((2, LANES, LANES), bf16),
    pltpu.SemaphoreType.DMA((3,)),
]


def own_kernel(o_ref, joined_ref, lines_ref, packed_ref, start_ref, joined, lines, sems):
    copies = table_copies(joined_ref, lines_ref, joined, lines, sems)
    own = to_planes(o_ref)
    fields = jnp.concatenate([own * own, own], axis=0)
    squares = wave_square()
    factors = jnp.concatenate([screening(squares), squares * (0.5 / CELLS)], axis=0)
    fields = twice_transformed(fields, factors, joined, lines, copies)
    square, kinetic = fields[:GRID], fields[GRID:]
    start = kinetic - MIXING * square * own
    parts, rows = packed_ref.shape[0], packed_ref.shape[2]
    packed_ref[:, 0] = o_ref[...].reshape(parts, rows, LANES)
    planes = rows // SPLIT
    for j in range(SPLIT):
        start_ref[pl.ds(j, GRID, stride=SPLIT), :] = start[:, j * LANES : (j + 1) * LANES]
        piece = square[:, j * LANES : (j + 1) * LANES]
        for k in range(parts):
            packed_ref[k, 1, pl.ds(j, planes, stride=SPLIT), :] = piece[k * planes : (k + 1) * planes]


def pair_kernel(x_ref, o_ref, start_ref, below, above, second, across, corner, joined_ref, lines_ref, out_ref, joined, lines, sems):
    copies = table_copies(joined_ref, lines_ref, joined, lines, sems)
    own = to_planes(o_ref)
    below, above, second, across, corner = (to_planes(ref) for ref in (below, above, second, across, corner))
    x = x_ref[0]
    partners = [
        jnp.where(x == 0, corner, below),
        jnp.where(x == GRID_X - 1, corner, above),
        second,
        across,
    ]
    fields = jnp.concatenate([own * partner for partner in partners], axis=0)
    factors = jnp.concatenate([screening(wave_square())] * 4, axis=0)
    fields = twice_transformed(fields, factors, joined, lines, copies)
    total = sum(fields[k * GRID : (k + 1) * GRID] * partners[k] for k in range(4))
    for j in range(SPLIT):
        rows = pl.ds(j, GRID, stride=SPLIT)
        out_ref[rows, :] = start_ref[rows, :] - MIXING * total[:, j * LANES : (j + 1) * LANES]


def spread_kernel(slabs_ref, out_ref):
    bands, rows = slabs_ref.shape[0], slabs_ref.shape[2]
    cells = bands * rows
    own = slabs_ref[:, 0].reshape(cells, LANES)
    square = jnp.sum(slabs_ref[:, 1], axis=0)
    for k in range(out_ref.shape[0]):
        out_ref[k, :cells] = own
        out_ref[k, cells:] = square


def overlap_kernel(gathered_ref, gradient_ref, packed_ref, square_ref, oh_ref, ol_ref):
    groups = gathered_ref.shape[0]
    rows = square_ref.shape[0]
    bands = gathered_ref.shape[1] // rows - 1
    cells = bands * rows
    square_ref[...] = jnp.sum(gathered_ref[:, cells:, :], axis=0)
    for k in range(groups):
        for c in range(rows):
            high, low = split(gathered_ref[k, pl.ds(c, bands, stride=rows), :])
            oh_ref[k * bands : (k + 1) * bands, c * LANES : (c + 1) * LANES] = high
            ol_ref[k * bands : (k + 1) * bands, c * LANES : (c + 1) * LANES] = low
    high, low = oh_ref[...], ol_ref[...]
    mixed = mmt(high, low)
    overlap = (mmt(high, high) + mixed + mixed.T) * (1.0 / CELLS)
    packed_ref[:, :rows] = gradient_ref[...].reshape(bands, rows, LANES)
    packed_ref[:, rows:] = overlap.reshape(bands, overlap.shape[0] // bands, LANES)


def correlate_kernel(slabs_ref, own_ref, potential_ref, square_ref, other_ref, oh_ref, ol_ref, corr_ref, g_out):
    bands, rows = g_out.shape[0], g_out.shape[1]
    local = potential_ref[...] + HARTREE_WEIGHT * (square_ref[...] + other_ref[...])
    g = slabs_ref[:, :rows] + local[None] * own_ref[:, 0]
    g_out[...] = g
    wide = jnp.concatenate([g[:, c, :] for c in range(rows)], axis=1)
    first = product(wide, oh_ref[...], ol_ref[...], mmt) * (1.0 / CELLS)
    overlap = jnp.sum(slabs_ref[:, rows:], axis=0)
    for k in range(bands):
        corr_ref[k, :bands] = first
        corr_ref[k, bands:] = overlap


def remove_kernel(corr_ref, g_ref, oh_ref, ol_ref, out_ref):
    bands, rows = g_ref.shape[0], g_ref.shape[1]
    first = jnp.sum(corr_ref[:, :bands], axis=0)
    overlap = corr_ref[:, bands:].reshape(LANES, LANES)
    s_high, s_low = split(overlap)
    weights = 2.0 * first - product(first, s_high, s_low, mm)
    taken = product(weights, oh_ref[...], ol_ref[...], mm)
    for c in range(rows):
        out_ref[:, c, :] = g_ref[:, c, :] - taken[:, c * LANES : (c + 1) * LANES]


def update_kernel(o_ref, residual_ref, updated_ref, out_ref):
    residual = residual_ref[...]
    out_ref[...] = residual
    updated_ref[...] = o_ref[...] - STEP_LENGTH * residual


def call(kernel, outs, args, name, tables=(), limit=40, flops=1 << 30, nbytes=1 << 23):
    single = not isinstance(outs, list)
    shapes = [outs] if single else outs
    result = pl.pallas_call(
        kernel,
        out_shape=[jax.ShapeDtypeStruct(s, t) for s, t in shapes],
        in_specs=[pl.BlockSpec(memory_space=pltpu.SMEM if a.dtype == jnp.int32 else pltpu.VMEM) for a in args]
        + [pl.BlockSpec(memory_space=pltpu.HBM)] * len(tables),
        out_specs=[pl.BlockSpec(memory_space=pltpu.VMEM)] * len(shapes),
        compiler_params=pltpu.CompilerParams(vmem_limit_bytes=limit << 20),
        cost_estimate=pl.CostEstimate(flops=flops, bytes_accessed=nbytes, transcendentals=0),
        scratch_shapes=TABLE_SCRATCH if tables else [],
        name=name,
    )(*args, *tables)
    return result[0] if single else result


def exchange(x, axes):
    return lax.all_to_all(x, axes, 0, 0, tiled=True)


def gather(x, axes):
    return exchange(jnp.broadcast_to(x[None], (size(axes),) + x.shape), axes)


def size(axes):
    return math.prod(lax.axis_size(a) for a in axes)


def shifted(x, axes, by):
    peers = size(axes)
    return lax.ppermute(x, axes, [(i, (i + by) % peers) for i in range(peers)])


def per_device(orbitals, potential):
    tables = constants()
    parts = size(SLAB)
    rows = ROWS // parts
    groups = size(GATHER)

    own = orbitals.reshape(ROWS, LANES)
    below, above, second = (shifted(own, ("x",), by) for by in (1, -1, 2))
    rings = size(BANDS[:-1])
    toward = [-1, -1, 1, 1]
    edge = lax.ppermute(
        own,
        BANDS,
        [(g * GRID_X + x, (g + toward[x]) % rings * GRID_X + x) for g in range(rings) for x in range(GRID_X)],
    )
    packed, start = call(
        own_kernel,
        [((parts, 2, rows, LANES), f32), ((ROWS, LANES), f32)],
        [own],
        "own_fields",
        tables,
        60,
    )
    packed, edge, below, above, second = lax.optimization_barrier((packed, edge, below, above, second))
    slabs = exchange(packed, SLAB)
    spread = call(spread_kernel, ((groups, (parts + 1) * rows, LANES), f32), [slabs], "spread")
    gathered = exchange(spread, GATHER)

    edge, spread = lax.optimization_barrier((edge, spread))
    across = shifted(edge, ("x",), 2)
    corner = lax.ppermute(edge, "x", [(0, GRID_X - 1), (GRID_X - 1, 0)])
    gradient = call(
        pair_kernel,
        ((ROWS, LANES), f32),
        [lax.axis_index("x").reshape(1), own, start, below, above, second, across, corner],
        "pair_fields",
        tables,
    )

    bands = parts * groups
    share = bands // parts
    packed, square, o_high, o_low = call(
        overlap_kernel,
        [
            ((parts, rows + share, LANES), f32),
            ((rows, LANES), f32),
            ((bands, rows * LANES), bf16),
            ((bands, rows * LANES), bf16),
        ],
        [gathered, gradient],
        "overlaps",
    )
    other = shifted(square, ("spin",), 1)
    slab_gradient = exchange(packed, SLAB)
    here = lax.axis_index(SLAB)
    slab_potential = lax.dynamic_slice_in_dim(potential.reshape(ROWS, LANES), here * rows, rows, 0)
    corr, slab_gradient = call(
        correlate_kernel,
        [((parts, parts + share, LANES), f32), ((parts, rows, LANES), f32)],
        [slab_gradient, slabs, slab_potential, square, other, o_high, o_low],
        "correlations",
    )
    corr = exchange(corr, SLAB)
    slab_residual = call(
        remove_kernel,
        ((parts, rows, LANES), f32),
        [corr, slab_gradient, o_high, o_low],
        "removal",
    )
    residual = exchange(slab_residual, SLAB).reshape(ROWS, LANES)
    updated, residual = call(
        update_kernel, [((ROWS, LANES), f32), ((ROWS, LANES), f32)], [own, residual], "update"
    )
    return updated.reshape(1, 1, CELLS), residual.reshape(1, 1, CELLS)


def solution(mesh):
    fine = Mesh(mesh.devices.reshape(2, 4, 4, 2, 4), ("spin",) + BANDS)
    spec = P("spin", BANDS, None)
    return jax.shard_map(
        per_device, mesh=fine, in_specs=(spec, P()), out_specs=(spec, spec), check_vma=False
    )
```

```python
import math

import jax
import jax.numpy as jnp
import ml_dtypes
import numpy as np
from jax import lax
from jax.experimental import pallas as pl
from jax.experimental.pallas import tpu as pltpu
from jax.sharding import Mesh
from jax.sharding import PartitionSpec as P

GRID = 32
PLANE = GRID * GRID
CELLS = GRID**3
LANES = 128
ROWS = CELLS // LANES
SPLIT = PLANE // LANES

SCREEN_SQUARE = 0.04
HARTREE_WEIGHT = 0.03125
MIXING = 0.25
STEP_LENGTH = 0.1

BANDS = ("y", "zh", "zl", "x")
GRID_X = 4
SLAB = ("zl", "x", "y")
GATHER = ("zh",)

f32 = jnp.float32
bf16 = jnp.bfloat16


def halves(value):
    high = value.astype(ml_dtypes.bfloat16)
    low = (value - high.astype(np.float64)).astype(ml_dtypes.bfloat16)
    return high, low


def constants():
    indices = np.arange(GRID)
    angles = (indices[:, None] * indices[None, :] % GRID) * (2.0 * math.pi / GRID)
    table = np.cos(angles) + np.sin(angles)
    joined = np.stack(halves(np.kron(table, table)))
    lines = np.stack(halves(np.kron(np.eye(4), table)))
    return jnp.asarray(joined), jnp.asarray(lines)


def wave_square():
    planes = lax.broadcasted_iota(jnp.int32, (GRID, PLANE), 0)
    cells = lax.broadcasted_iota(jnp.int32, (GRID, PLANE), 1)

    def square(index):
        wave = jnp.where(index < GRID // 2, index, index - GRID).astype(f32) * (math.pi / GRID)
        return wave * wave

    return square(planes) + square(cells // GRID) + square(cells % GRID)


def screening(squares):
    kept = squares > 0
    return jnp.where(kept, 1.0 / jnp.where(kept, squares + SCREEN_SQUARE, 1.0), 0.0) * (1.0 / CELLS)


def split(value):
    high = value.astype(bf16)
    return high, (value - high.astype(f32)).astype(bf16)


def mm(left, right):
    return lax.dot_general(left, right, (((1,), (0,)), ((), ())), preferred_element_type=f32)


def mmt(left, right):
    return lax.dot_general(left, right, (((1,), (1,)), ((), ())), preferred_element_type=f32)


def product(left, right_high, right_low, multiply):
    high, low = split(left)
    rows = left.shape[0]
    both = multiply(jnp.concatenate([high, low], axis=0), right_high)
    return both[:rows] + both[rows:] + multiply(high, right_low)


def along_line(value, lines):
    rows = value.shape[0]
    line_high, line_low = lines[0, :rows, :rows], lines[1, :rows, :rows]
    high, low = split(value)
    both = mm(jnp.concatenate([line_high, line_low], axis=0), high)
    return both[:rows] + both[rows:] + mm(line_high, low)


def twice_transformed(fields, factors, joined, lines, copies):
    high, low = split(fields)
    rows = fields.shape[0]
    copies[0].wait()
    both = mm(jnp.concatenate([high, low], axis=0), joined[0])
    copies[1].wait()
    value = both[:rows] + both[rows:] + mm(high, joined[1])
    copies[2].wait()
    value = along_line(value, lines) * factors
    return along_line(product(value, joined[0], joined[1], mm), lines)


def to_planes(ref):
    return jnp.concatenate([ref[pl.ds(j, GRID, stride=SPLIT), :] for j in range(SPLIT)], axis=1)


def table_copies(joined_ref, lines_ref, joined, lines, sems):
    copies = [
        pltpu.make_async_copy(joined_ref.at[0], joined.at[0], sems.at[0]),
        pltpu.make_async_copy(joined_ref.at[1], joined.at[1], sems.at[1]),
        pltpu.make_async_copy(lines_ref, lines, sems.at[2]),
    ]
    for copy in copies:
        copy.start()
    return copies


TABLE_SCRATCH = [
    pltpu.VMEM((2, PLANE, PLANE), bf16),
    pltpu.VMEM((2, LANES, LANES), bf16),
    pltpu.SemaphoreType.DMA((3,)),
]


def own_kernel(o_ref, joined_ref, lines_ref, packed_ref, start_ref, joined, lines, sems):
    copies = table_copies(joined_ref, lines_ref, joined, lines, sems)
    own = to_planes(o_ref)
    fields = jnp.concatenate([own * own, own], axis=0)
    squares = wave_square()
    factors = jnp.concatenate([screening(squares), squares * (0.5 / CELLS)], axis=0)
    fields = twice_transformed(fields, factors, joined, lines, copies)
    square, kinetic = fields[:GRID], fields[GRID:]
    start = kinetic - MIXING * square * own
    parts, rows = packed_ref.shape[0], packed_ref.shape[2]
    packed_ref[:, 0] = o_ref[...].reshape(parts, rows, LANES)
    planes = rows // SPLIT
    for j in range(SPLIT):
        start_ref[pl.ds(j, GRID, stride=SPLIT), :] = start[:, j * LANES : (j + 1) * LANES]
        piece = square[:, j * LANES : (j + 1) * LANES]
        for k in range(parts):
            packed_ref[k, 1, pl.ds(j, planes, stride=SPLIT), :] = piece[k * planes : (k + 1) * planes]


def pair_kernel(x_ref, o_ref, start_ref, below, above, second, across, corner, joined_ref, lines_ref, out_ref, joined, lines, sems):
    copies = table_copies(joined_ref, lines_ref, joined, lines, sems)
    own = to_planes(o_ref)
    below, above, second, across, corner = (to_planes(ref) for ref in (below, above, second, across, corner))
    x = x_ref[0]
    partners = [
        jnp.where(x == 0, corner, below),
        jnp.where(x == GRID_X - 1, corner, above),
        second,
        across,
    ]
    fields = jnp.concatenate([own * partner for partner in partners], axis=0)
    factors = jnp.concatenate([screening(wave_square())] * 4, axis=0)
    fields = twice_transformed(fields, factors, joined, lines, copies)
    total = sum(fields[k * GRID : (k + 1) * GRID] * partners[k] for k in range(4))
    for j in range(SPLIT):
        rows = pl.ds(j, GRID, stride=SPLIT)
        out_ref[rows, :] = start_ref[rows, :] - MIXING * total[:, j * LANES : (j + 1) * LANES]


def spread_kernel(slabs_ref, out_ref):
    bands, rows = slabs_ref.shape[0], slabs_ref.shape[2]
    cells = bands * rows
    own = slabs_ref[:, 0].reshape(cells, LANES)
    square = jnp.sum(slabs_ref[:, 1], axis=0)
    for k in range(out_ref.shape[0]):
        out_ref[k, :cells] = own
        out_ref[k, cells:] = square


def overlap_kernel(gathered_ref, gradient_ref, packed_ref, square_ref, oh_ref, ol_ref):
    groups = gathered_ref.shape[0]
    rows = square_ref.shape[0]
    bands = gathered_ref.shape[1] // rows - 1
    cells = bands * rows
    square_ref[...] = jnp.sum(gathered_ref[:, cells:, :], axis=0)
    for k in range(groups):
        for c in range(rows):
            high, low = split(gathered_ref[k, pl.ds(c, bands, stride=rows), :])
            oh_ref[k * bands : (k + 1) * bands, c * LANES : (c + 1) * LANES] = high
            ol_ref[k * bands : (k + 1) * bands, c * LANES : (c + 1) * LANES] = low
    high, low = oh_ref[...], ol_ref[...]
    mixed = mmt(high, low)
    overlap = (mmt(high, high) + mixed + mixed.T) * (1.0 / CELLS)
    packed_ref[:, :rows] = gradient_ref[...].reshape(bands, rows, LANES)
    packed_ref[:, rows:] = overlap.reshape(bands, overlap.shape[0] // bands, LANES)


def correlate_kernel(slabs_ref, own_ref, potential_ref, square_ref, other_ref, oh_ref, ol_ref, corr_ref, g_out):
    bands, rows = g_out.shape[0], g_out.shape[1]
    local = potential_ref[...] + HARTREE_WEIGHT * (square_ref[...] + other_ref[...])
    g = slabs_ref[:, :rows] + local[None] * own_ref[:, 0]
    g_out[...] = g
    wide = jnp.concatenate([g[:, c, :] for c in range(rows)], axis=1)
    first = product(wide, oh_ref[...], ol_ref[...], mmt) * (1.0 / CELLS)
    overlap = jnp.sum(slabs_ref[:, rows:], axis=0)
    for k in range(bands):
        corr_ref[k, :bands] = first
        corr_ref[k, bands:] = overlap


def remove_kernel(corr_ref, g_ref, oh_ref, ol_ref, out_ref):
    bands, rows = g_ref.shape[0], g_ref.shape[1]
    first = jnp.sum(corr_ref[:, :bands], axis=0)
    overlap = corr_ref[:, bands:].reshape(LANES, LANES)
    s_high, s_low = split(overlap)
    weights = 2.0 * first - product(first, s_high, s_low, mm)
    taken = product(weights, oh_ref[...], ol_ref[...], mm)
    for c in range(rows):
        out_ref[:, c, :] = g_ref[:, c, :] - taken[:, c * LANES : (c + 1) * LANES]


def update_kernel(o_ref, residual_ref, updated_ref, out_ref):
    residual = residual_ref[...]
    out_ref[...] = residual
    updated_ref[...] = o_ref[...] - STEP_LENGTH * residual


def call(kernel, outs, args, name, tables=(), limit=40, flops=1 << 30, nbytes=1 << 23):
    single = not isinstance(outs, list)
    shapes = [outs] if single else outs
    result = pl.pallas_call(
        kernel,
        out_shape=[jax.ShapeDtypeStruct(s, t) for s, t in shapes],
        in_specs=[pl.BlockSpec(memory_space=pltpu.SMEM if a.dtype == jnp.int32 else pltpu.VMEM) for a in args]
        + [pl.BlockSpec(memory_space=pltpu.HBM)] * len(tables),
        out_specs=[pl.BlockSpec(memory_space=pltpu.VMEM)] * len(shapes),
        compiler_params=pltpu.CompilerParams(vmem_limit_bytes=limit << 20),
        cost_estimate=pl.CostEstimate(flops=flops, bytes_accessed=nbytes, transcendentals=0),
        scratch_shapes=TABLE_SCRATCH if tables else [],
        name=name,
    )(*args, *tables)
    return result[0] if single else result


def exchange(x, axes):
    return lax.all_to_all(x, axes, 0, 0, tiled=True)


def gather(x, axes):
    return exchange(jnp.broadcast_to(x[None], (size(axes),) + x.shape), axes)


def size(axes):
    return math.prod(lax.axis_size(a) for a in axes)


def shifted(x, axes, by):
    peers = size(axes)
    return lax.ppermute(x, axes, [(i, (i + by) % peers) for i in range(peers)])


def per_device(orbitals, potential):
    tables = constants()
    parts = size(SLAB)
    rows = ROWS // parts
    groups = size(GATHER)

    own = orbitals.reshape(ROWS, LANES)
    below, above, second = (shifted(own, ("x",), by) for by in (1, -1, 2))
    rings = size(BANDS[:-1])
    toward = [-1, -1, 1, 1]
    edge = lax.ppermute(
        own,
        BANDS,
        [(g * GRID_X + x, (g + toward[x]) % rings * GRID_X + x) for g in range(rings) for x in range(GRID_X)],
    )
    packed, start = call(
        own_kernel,
        [((parts, 2, rows, LANES), f32), ((ROWS, LANES), f32)],
        [own],
        "own_fields",
        tables,
        60,
    )
    packed, edge, below, above, second = lax.optimization_barrier((packed, edge, below, above, second))
    slabs = exchange(packed, SLAB)
    spread = call(spread_kernel, ((groups, (parts + 1) * rows, LANES), f32), [slabs], "spread")
    gathered = exchange(spread, GATHER)

    edge, spread = lax.optimization_barrier((edge, spread))
    across = shifted(edge, ("x",), 2)
    corner = lax.ppermute(edge, "x", [(i, GRID_X - 1 - i) for i in range(GRID_X)])
    gradient = call(
        pair_kernel,
        ((ROWS, LANES), f32),
        [lax.axis_index("x").reshape(1), own, start, below, above, second, across, corner],
        "pair_fields",
        tables,
    )

    bands = parts * groups
    share = bands // parts
    packed, square, o_high, o_low = call(
        overlap_kernel,
        [
            ((parts, rows + share, LANES), f32),
            ((rows, LANES), f32),
            ((bands, rows * LANES), bf16),
            ((bands, rows * LANES), bf16),
        ],
        [gathered, gradient],
        "overlaps",
    )
    other = shifted(square, ("spin",), 1)
    slab_gradient = exchange(packed, SLAB)
    here = lax.axis_index(SLAB)
    slab_potential = lax.dynamic_slice_in_dim(potential.reshape(ROWS, LANES), here * rows, rows, 0)
    corr, slab_gradient = call(
        correlate_kernel,
        [((parts, parts + share, LANES), f32), ((parts, rows, LANES), f32)],
        [slab_gradient, slabs, slab_potential, square, other, o_high, o_low],
        "correlations",
    )
    corr = exchange(corr, SLAB)
    slab_residual = call(
        remove_kernel,
        ((parts, rows, LANES), f32),
        [corr, slab_gradient, o_high, o_low],
        "removal",
    )
    residual = exchange(slab_residual, SLAB).reshape(ROWS, LANES)
    updated, residual = call(
        update_kernel, [((ROWS, LANES), f32), ((ROWS, LANES), f32)], [own, residual], "update"
    )
    return updated.reshape(1, 1, CELLS), residual.reshape(1, 1, CELLS)


def solution(mesh):
    fine = Mesh(mesh.devices.reshape(2, 4, 4, 2, 4), ("spin",) + BANDS)
    spec = P("spin", BANDS, None)
    return jax.shard_map(
        per_device, mesh=fine, in_specs=(spec, P()), out_specs=(spec, spec), check_vma=False
    )
```

```python
import math

import jax
import jax.numpy as jnp
import ml_dtypes
import numpy as np
from jax import lax
from jax.experimental import pallas as pl
from jax.experimental.pallas import tpu as pltpu
from jax.sharding import Mesh
from jax.sharding import PartitionSpec as P

GRID = 32
PLANE = GRID * GRID
CELLS = GRID**3
LANES = 128
ROWS = CELLS // LANES
SPLIT = PLANE // LANES

SCREEN_SQUARE = 0.04
HARTREE_WEIGHT = 0.03125
MIXING = 0.25
STEP_LENGTH = 0.1

BANDS = ("y", "zh", "zl", "x")
GRID_X = 4
SLAB = ("zl", "x", "y")
GATHER = ("zh",)

f32 = jnp.float32
bf16 = jnp.bfloat16


def halves(value):
    high = value.astype(ml_dtypes.bfloat16)
    low = (value - high.astype(np.float64)).astype(ml_dtypes.bfloat16)
    return high, low


def constants():
    indices = np.arange(GRID)
    angles = (indices[:, None] * indices[None, :] % GRID) * (2.0 * math.pi / GRID)
    table = np.cos(angles) + np.sin(angles)
    joined = np.stack(halves(np.kron(table, table)))
    lines = np.stack(halves(np.kron(np.eye(4), table)))
    return jnp.asarray(joined), jnp.asarray(lines)


def wave_square():
    planes = lax.broadcasted_iota(jnp.int32, (GRID, PLANE), 0)
    cells = lax.broadcasted_iota(jnp.int32, (GRID, PLANE), 1)

    def square(index):
        wave = jnp.where(index < GRID // 2, index, index - GRID).astype(f32) * (math.pi / GRID)
        return wave * wave

    return square(planes) + square(cells // GRID) + square(cells % GRID)


def screening(squares):
    kept = squares > 0
    return jnp.where(kept, 1.0 / jnp.where(kept, squares + SCREEN_SQUARE, 1.0), 0.0) * (1.0 / CELLS)


def split(value):
    high = value.astype(bf16)
    return high, (value - high.astype(f32)).astype(bf16)


def mm(left, right):
    return lax.dot_general(left, right, (((1,), (0,)), ((), ())), preferred_element_type=f32)


def mmt(left, right):
    return lax.dot_general(left, right, (((1,), (1,)), ((), ())), preferred_element_type=f32)


def product(left, right_high, right_low, multiply):
    high, low = split(left)
    rows = left.shape[0]
    both = multiply(jnp.concatenate([high, low], axis=0), right_high)
    return both[:rows] + both[rows:] + multiply(high, right_low)


def along_line(value, lines):
    rows = value.shape[0]
    line_high, line_low = lines[0, :rows, :rows], lines[1, :rows, :rows]
    high, low = split(value)
    both = mm(jnp.concatenate([line_high, line_low], axis=0), high)
    return both[:rows] + both[rows:] + mm(line_high, low)


def twice_transformed(fields, factors, joined, lines, copies=()):
    for copy in copies[:1]:
        copy.wait()
    value = along_line(fields, lines)
    high, low = split(value)
    rows = fields.shape[0]
    for copy in copies[1:2]:
        copy.wait()
    both = mm(jnp.concatenate([high, low], axis=0), joined[0])
    for copy in copies[2:]:
        copy.wait()
    value = (both[:rows] + both[rows:] + mm(high, joined[1])) * factors
    return along_line(product(value, joined[0], joined[1], mm), lines)


def to_planes(ref):
    return jnp.concatenate([ref[pl.ds(j, GRID, stride=SPLIT), :] for j in range(SPLIT)], axis=1)


def table_copies(joined_ref, lines_ref, joined, lines, sems):
    copies = [
        pltpu.make_async_copy(lines_ref, lines, sems.at[0]),
        pltpu.make_async_copy(joined_ref.at[0], joined.at[0], sems.at[1]),
        pltpu.make_async_copy(joined_ref.at[1], joined.at[1], sems.at[2]),
    ]
    for copy in copies:
        copy.start()
    return copies


TABLE_SCRATCH = [
    pltpu.VMEM((2, PLANE, PLANE), bf16),
    pltpu.VMEM((2, LANES, LANES), bf16),
    pltpu.SemaphoreType.DMA((3,)),
]


def own_kernel(o_ref, joined_ref, lines_ref, packed_ref, start_ref, joined, lines, sems):
    copies = table_copies(joined_ref, lines_ref, joined, lines, sems)
    own = to_planes(o_ref)
    fields = jnp.concatenate([own * own, own], axis=0)
    squares = wave_square()
    factors = jnp.concatenate([screening(squares), squares * (0.5 / CELLS)], axis=0)
    fields = twice_transformed(fields, factors, joined, lines, copies)
    square, kinetic = fields[:GRID], fields[GRID:]
    start = kinetic - MIXING * square * own
    parts, rows = packed_ref.shape[0], packed_ref.shape[2]
    packed_ref[:, 0] = o_ref[...].reshape(parts, rows, LANES)
    planes = rows // SPLIT
    for j in range(SPLIT):
        start_ref[pl.ds(j, GRID, stride=SPLIT), :] = start[:, j * LANES : (j + 1) * LANES]
        piece = square[:, j * LANES : (j + 1) * LANES]
        for k in range(parts):
            packed_ref[k, 1, pl.ds(j, planes, stride=SPLIT), :] = piece[k * planes : (k + 1) * planes]


def pair_kernel(x_ref, o_ref, start_ref, below, above, second, across, corner, joined, lines, out_ref):
    own = to_planes(o_ref)
    below, above, second, across, corner = (to_planes(ref) for ref in (below, above, second, across, corner))
    x = x_ref[0]
    partners = [
        jnp.where(x == 0, corner, below),
        jnp.where(x == GRID_X - 1, corner, above),
        second,
        across,
    ]
    fields = jnp.concatenate([own * partner for partner in partners], axis=0)
    factors = jnp.concatenate([screening(wave_square())] * 4, axis=0)
    fields = twice_transformed(fields, factors, joined, lines)
    total = sum(fields[k * GRID : (k + 1) * GRID] * partners[k] for k in range(4))
    for j in range(SPLIT):
        rows = pl.ds(j, GRID, stride=SPLIT)
        out_ref[rows, :] = start_ref[rows, :] - MIXING * total[:, j * LANES : (j + 1) * LANES]


def spread_kernel(slabs_ref, out_ref):
    bands, rows = slabs_ref.shape[0], slabs_ref.shape[2]
    cells = bands * rows
    own = slabs_ref[:, 0].reshape(cells, LANES)
    square = jnp.sum(slabs_ref[:, 1], axis=0)
    for k in range(out_ref.shape[0]):
        out_ref[k, :cells] = own
        out_ref[k, cells:] = square


def overlap_kernel(gathered_ref, gradient_ref, packed_ref, square_ref, oh_ref, ol_ref):
    groups = gathered_ref.shape[0]
    rows = square_ref.shape[0]
    bands = gathered_ref.shape[1] // rows - 1
    cells = bands * rows
    square_ref[...] = jnp.sum(gathered_ref[:, cells:, :], axis=0)
    for k in range(groups):
        for c in range(rows):
            high, low = split(gathered_ref[k, pl.ds(c, bands, stride=rows), :])
            oh_ref[k * bands : (k + 1) * bands, c * LANES : (c + 1) * LANES] = high
            ol_ref[k * bands : (k + 1) * bands, c * LANES : (c + 1) * LANES] = low
    high, low = oh_ref[...], ol_ref[...]
    mixed = mmt(high, low)
    overlap = (mmt(high, high) + mixed + mixed.T) * (1.0 / CELLS)
    packed_ref[:, :rows] = gradient_ref[...].reshape(bands, rows, LANES)
    packed_ref[:, rows:] = overlap.reshape(bands, overlap.shape[0] // bands, LANES)


def correlate_kernel(slabs_ref, own_ref, potential_ref, square_ref, other_ref, oh_ref, ol_ref, corr_ref, g_out):
    bands, rows = g_out.shape[0], g_out.shape[1]
    local = potential_ref[...] + HARTREE_WEIGHT * (square_ref[...] + other_ref[...])
    g = slabs_ref[:, :rows] + local[None] * own_ref[:, 0]
    g_out[...] = g
    wide = jnp.concatenate([g[:, c, :] for c in range(rows)], axis=1)
    first = product(wide, oh_ref[...], ol_ref[...], mmt) * (1.0 / CELLS)
    overlap = jnp.sum(slabs_ref[:, rows:], axis=0)
    for k in range(bands):
        corr_ref[k, :bands] = first
        corr_ref[k, bands:] = overlap


def remove_kernel(corr_ref, g_ref, oh_ref, ol_ref, out_ref):
    bands, rows = g_ref.shape[0], g_ref.shape[1]
    first = jnp.sum(corr_ref[:, :bands], axis=0)
    overlap = corr_ref[:, bands:].reshape(LANES, LANES)
    s_high, s_low = split(overlap)
    weights = 2.0 * first - product(first, s_high, s_low, mm)
    taken = product(weights, oh_ref[...], ol_ref[...], mm)
    for c in range(rows):
        out_ref[:, c, :] = g_ref[:, c, :] - taken[:, c * LANES : (c + 1) * LANES]


def update_kernel(o_ref, residual_ref, updated_ref, out_ref):
    residual = residual_ref[...]
    out_ref[...] = residual
    updated_ref[...] = o_ref[...] - STEP_LENGTH * residual


def call(kernel, outs, args, name, tables=(), limit=40, flops=1 << 30, nbytes=1 << 23):
    single = not isinstance(outs, list)
    shapes = [outs] if single else outs
    result = pl.pallas_call(
        kernel,
        out_shape=[jax.ShapeDtypeStruct(s, t) for s, t in shapes],
        in_specs=[pl.BlockSpec(memory_space=pltpu.SMEM if a.dtype == jnp.int32 else pltpu.VMEM) for a in args]
        + [pl.BlockSpec(memory_space=pltpu.HBM)] * len(tables),
        out_specs=[pl.BlockSpec(memory_space=pltpu.VMEM)] * len(shapes),
        compiler_params=pltpu.CompilerParams(vmem_limit_bytes=limit << 20),
        cost_estimate=pl.CostEstimate(flops=flops, bytes_accessed=nbytes, transcendentals=0),
        scratch_shapes=TABLE_SCRATCH if tables else [],
        name=name,
    )(*args, *tables)
    return result[0] if single else result


def exchange(x, axes):
    return lax.all_to_all(x, axes, 0, 0, tiled=True)


def gather(x, axes):
    return exchange(jnp.broadcast_to(x[None], (size(axes),) + x.shape), axes)


def size(axes):
    return math.prod(lax.axis_size(a) for a in axes)


def shifted(x, axes, by):
    peers = size(axes)
    return lax.ppermute(x, axes, [(i, (i + by) % peers) for i in range(peers)])


def per_device(orbitals, potential):
    tables = constants()
    parts = size(SLAB)
    rows = ROWS // parts
    groups = size(GATHER)

    own = orbitals.reshape(ROWS, LANES)
    below, above, second = (shifted(own, ("x",), by) for by in (1, -1, 2))
    rings = size(BANDS[:-1])
    toward = [-1, -1, 1, 1]
    edge = lax.ppermute(
        own,
        BANDS,
        [(g * GRID_X + x, (g + toward[x]) % rings * GRID_X + x) for g in range(rings) for x in range(GRID_X)],
    )
    packed, start = call(
        own_kernel,
        [((parts, 2, rows, LANES), f32), ((ROWS, LANES), f32)],
        [own],
        "own_fields",
        tables,
        60,
    )
    packed, edge, below, above, second = lax.optimization_barrier((packed, edge, below, above, second))
    slabs = exchange(packed, SLAB)
    spread = call(spread_kernel, ((groups, (parts + 1) * rows, LANES), f32), [slabs], "spread")
    gathered = exchange(spread, GATHER)

    edge, spread = lax.optimization_barrier((edge, spread))
    across = shifted(edge, ("x",), 2)
    corner = lax.ppermute(edge, "x", [(i, GRID_X - 1 - i) for i in range(GRID_X)])
    gradient = call(
        pair_kernel,
        ((ROWS, LANES), f32),
        [lax.axis_index("x").reshape(1), own, start, below, above, second, across, corner, *tables],
        "pair_fields",
    )

    bands = parts * groups
    share = bands // parts
    packed, square, o_high, o_low = call(
        overlap_kernel,
        [
            ((parts, rows + share, LANES), f32),
            ((rows, LANES), f32),
            ((bands, rows * LANES), bf16),
            ((bands, rows * LANES), bf16),
        ],
        [gathered, gradient],
        "overlaps",
    )
    other = shifted(square, ("spin",), 1)
    slab_gradient = exchange(packed, SLAB)
    here = lax.axis_index(SLAB)
    slab_potential = lax.dynamic_slice_in_dim(potential.reshape(ROWS, LANES), here * rows, rows, 0)
    corr, slab_gradient = call(
        correlate_kernel,
        [((parts, parts + share, LANES), f32), ((parts, rows, LANES), f32)],
        [slab_gradient, slabs, slab_potential, square, other, o_high, o_low],
        "correlations",
    )
    corr = exchange(corr, SLAB)
    slab_residual = call(
        remove_kernel,
        ((parts, rows, LANES), f32),
        [corr, slab_gradient, o_high, o_low],
        "removal",
    )
    residual = exchange(slab_residual, SLAB).reshape(ROWS, LANES)
    updated, residual = call(
        update_kernel, [((ROWS, LANES), f32), ((ROWS, LANES), f32)], [own, residual], "update"
    )
    return updated.reshape(1, 1, CELLS), residual.reshape(1, 1, CELLS)


def solution(mesh):
    fine = Mesh(mesh.devices.reshape(2, 4, 4, 2, 4), ("spin",) + BANDS)
    spec = P("spin", BANDS, None)
    return jax.shard_map(
        per_device, mesh=fine, in_specs=(spec, P()), out_specs=(spec, spec), check_vma=False
    )
```
